32 devices in a mesh: fsdp: 32 (over z, y, x, core).
Axes of the slice: x: 2, y: 2, z: 4, core: 2. Of those that a mesh axis runs over, the one named last changes fastest.
Arguments:
- hidden_in: bfloat16 [8192, 768], P('fsdp'), may hold values from -6 to 6
- cotangent: bfloat16 [8192, 768], P('fsdp'), may hold values from -6 to 6
- seq_lengths: int32 [63], replicated, may hold values from 1 to 256, as said below
- seq_owner: int32 [63], replicated, may hold values from 0 to 31, as said below
- seq_start: int32 [63], replicated, may hold values from 0 to 255, as said below
- first_gain: bfloat16 [768], P('fsdp'), may hold values from 0.25 to 1.75
- first_shift: bfloat16 [768], P('fsdp'), may hold values from -1.75 to 1.75
- qkv_weight: bfloat16 [768, 2304], P('fsdp'), may hold values from -0.21875 to 0.21875
- qv_bias: bfloat16 [1536], P('fsdp'), may hold values from -1.75 to 1.75
- proj_weight: bfloat16 [768, 768], P('fsdp'), may hold values from -0.625 to 0.625
- proj_bias: bfloat16 [768], P('fsdp'), may hold values from -1.75 to 1.75
- second_gain: bfloat16 [768], P('fsdp'), may hold values from 0.25 to 1.75
- second_shift: bfloat16 [768], P('fsdp'), may hold values from -1.75 to 1.75
- up_weight: bfloat16 [768, 3072], P('fsdp'), may hold values from -0.21875 to 0.21875
- up_bias: bfloat16 [3072], P('fsdp'), may hold values from -1.75 to 1.75
- down_weight: bfloat16 [3072, 768], P('fsdp'), may hold values from -0.109375 to 0.109375
- down_bias: bfloat16 [768], P('fsdp'), may hold values from -1.75 to 1.75
Outputs:
- layer_out: bfloat16 [8192, 768], P('fsdp')
- input_grad: float32 [8192, 768], P('fsdp')
- first_gain_grad: float32 [768], P('fsdp')
- first_shift_grad: float32 [768], P('fsdp')
- qkv_weight_grad: float32 [768, 2304], P('fsdp')
- qv_bias_grad: float32 [1536], P('fsdp')
- proj_weight_grad: float32 [768, 768], P('fsdp')
- proj_bias_grad: float32 [768], P('fsdp')
- second_gain_grad: float32 [768], P('fsdp')
- second_shift_grad: float32 [768], P('fsdp')
- up_weight_grad: float32 [768, 3072], P('fsdp')
- up_bias_grad: float32 [3072], P('fsdp')
- down_weight_grad: float32 [3072, 768], P('fsdp')
- down_bias_grad: float32 [768], P('fsdp')
The draws below stay inside these ranges and needn't reach their ends.
Inputs may be any that keep to these rules, and one draw needn't show every extreme that they name: `seq_lengths`: every device holds one or two sequences, packed from its slot 0 upward in order of their numbers; slots after them are empty. Exactly one device holds a single sequence filling all 256 slots. `seq_owner`: every device owns at least one sequence. `seq_start`: A sequence starts where the previous sequence of its device ends, or at 0.
All inputs are finite; a program needn't handle non-finite values.
Results may differ from the reference program's by a relative error of at most 0.011.
Values may be sent and summed in bfloat16 or wider, within the bound.
A program may use at most 192 MiB of HBM per device.

```python
import jax
import jax.numpy as jnp
from jax import lax

D = 768
H = 12
HD = 64
FF = 3072
TOK_DEV = 256
TOKENS = 8192
N_FSDP = 32


def seq_layout(key):
    key_perm, key_level, key_first = jax.random.split(key, 3)
    shuffled = jax.random.permutation(key_perm, N_FSDP).astype(jnp.int32)
    devices = jnp.arange(N_FSDP, dtype=jnp.int32)
    single = shuffled[N_FSDP - 1]
    forced = shuffled[0]
    level = jax.random.randint(key_level, (N_FSDP,), 0, 3)
    filled = jnp.where(level == 0, TOK_DEV, jnp.where(level == 1, TOK_DEV // 2, TOK_DEV // 4)).astype(jnp.int32)
    filled = jnp.where((devices == single) | (devices == forced), TOK_DEV, filled)
    first_len = jax.random.randint(key_first, (N_FSDP,), 1, filled).astype(jnp.int32)
    first_len = jnp.where(devices == forced, TOK_DEV - 1, first_len)
    first_len = jnp.where(devices == single, TOK_DEV, first_len)
    extra_owner = shuffled[:N_FSDP - 1]
    extra_len = filled[extra_owner] - first_len[extra_owner]
    lengths = jnp.concatenate([first_len, extra_len]).astype(jnp.int32)
    owners = jnp.concatenate([devices, extra_owner]).astype(jnp.int32)
    starts = jnp.concatenate([jnp.zeros((N_FSDP,), jnp.int32), first_len[extra_owner]]).astype(jnp.int32)
    return (lengths, owners, starts)


def draw_seq_lengths(key, part):
    shared = seq_layout(key)
    return shared[0]


def draw_seq_owner(key, part):
    shared = seq_layout(key)
    return shared[1]


def draw_seq_start(key, part):
    shared = seq_layout(key)
    return shared[2]


def raised(drawn, key, source, target, shards_of, factor):
    def block_of(position):
        return (jnp.arange(drawn.shape[position]) // (drawn.shape[position] // shards_of)).reshape((-1,) + (1,) * (drawn.ndim - 1 - position))

    near = jax.random.permutation(key, shards_of)[block_of(target)]
    other_side = (block_of(target) + shards_of // 2) % shards_of
    return jnp.where((block_of(source) == near) | (block_of(source) == other_side), factor * drawn, drawn)


def levels(own_key, dims, cuts, low, high):
    def one(axis_at, blocks):
        steps = jax.random.uniform(jax.random.fold_in(jax.random.fold_in(own_key, 6), axis_at), (blocks,), jnp.float32, low / len(cuts), high / len(cuts))
        return jnp.repeat(jnp.exp(steps), dims[axis_at] // blocks).reshape((-1,) + (1,) * (len(dims) - axis_at - 1))

    level = one(*cuts[0])
    for cut in cuts[1:]:
        level = level * one(*cut)
    return level


def noise(key, extent, width, limit, cuts=(), kind=jnp.bfloat16):
    level = levels(key, extent, cuts, -0.22, 0.18) if cuts else 1.0
    values = jax.random.normal(key, extent, jnp.float32) * width * level
    return jnp.minimum(jnp.maximum(values, -limit), limit).astype(kind)


def noise_with(own_key, extent, spread, most, cuts, heavy, held_as=jnp.bfloat16):
    entries = spread * jax.random.normal(own_key, extent, jnp.float32)
    if cuts:
        entries = entries * levels(own_key, extent, cuts, -0.22, 0.18)
    return jnp.clip(raised(entries, jax.random.fold_in(own_key, 3), *heavy), -most, most).astype(held_as)


def setup_inputs(seed: int = 0) -> dict:
    key_list = jax.random.split(jax.random.key(seed), 18)
    hidden_in = noise(key_list[0], (TOKENS, D), 1.0, 6.0, ((0, 32),))
    cotangent = noise_with(key_list[1], (TOKENS, D), 1.0, 6.0, ((0, 32),), (0, 1, 32, 2.75))
    seq_lengths = draw_seq_lengths(jax.random.fold_in(key_list[17], 71), 0)
    seq_owner = draw_seq_owner(jax.random.fold_in(key_list[17], 71), 0)
    seq_start = draw_seq_start(jax.random.fold_in(key_list[17], 71), 0)
    first_gain = jnp.clip(1.0 + 0.15 * jax.random.normal(key_list[5], (D,), jnp.float32), 0.25, 1.75).astype(jnp.bfloat16)
    first_shift = noise(key_list[6], (D,), 0.3, 1.75, ((0, 32),))
    qkv_weight = noise(key_list[7], (D, 3 * D), D ** -0.5, 0.21875, ((0, 32),))
    qv_bias = noise(key_list[8], (2 * D,), 0.3, 1.75, ((0, 32),))
    proj_weight = noise(key_list[9], (D, D), (D // 8) ** -0.5, 0.625, ((0, 32),))
    proj_bias = noise(key_list[10], (D,), 0.3, 1.75, ((0, 32),))
    second_gain = jnp.clip(1.0 + 0.15 * jax.random.normal(key_list[11], (D,), jnp.float32), 0.25, 1.75).astype(jnp.bfloat16)
    second_shift = noise(key_list[12], (D,), 0.3, 1.75, ((0, 32),))
    up_weight = noise(key_list[13], (D, FF), D ** -0.5, 0.21875, ((0, 32),))
    up_bias = noise(key_list[14], (FF,), 0.3, 1.75, ((0, 32),))
    down_weight = noise(key_list[15], (FF, D), FF ** -0.5, 0.109375, ((0, 32),))
    down_bias = noise(key_list[16], (D,), 0.3, 1.75, ((0, 32),))
    return dict(hidden_in=hidden_in, cotangent=cotangent, seq_lengths=seq_lengths, seq_owner=seq_owner, seq_start=seq_start, first_gain=first_gain, first_shift=first_shift, qkv_weight=qkv_weight, qv_bias=qv_bias, proj_weight=proj_weight, proj_bias=proj_bias, second_gain=second_gain, second_shift=second_shift, up_weight=up_weight, up_bias=up_bias, down_weight=down_weight, down_bias=down_bias)


@jax.custom_vjp
def low(v):
    return lax.optimization_barrier(v.astype(jnp.bfloat16)).astype(jnp.float32)

@jax.custom_vjp
def low_back(v):
    return v

def low_keep(v):
    return (low(v), None)

def low_pass(kept, grad):
    return (grad,)

def back_keep(v):
    return (v, None)

def back_low(kept, grad):
    return (low(grad),)
low.defvjp(low_keep, low_pass)
low_back.defvjp(back_keep, back_low)

def rounded_both(value):
    return low(low_back(value))

def layer_norm(values, gain, shift):
    average = lax.optimization_barrier(jnp.mean(values, axis=-1, keepdims=True))
    centered = values - average
    variance = lax.optimization_barrier(jnp.mean(centered * centered, axis=-1, keepdims=True))
    return centered * lax.rsqrt(variance + 1e-05) * gain + shift

def slot_layout(lengths, owners, starts, device, row_count):
    slot_ids = jnp.arange(row_count, dtype=jnp.int32)[:, None]
    inside = (owners[None, :] == device) & (slot_ids >= starts[None, :]) & (slot_ids < (starts + lengths)[None, :])
    seq_ids = jnp.arange(lengths.shape[0], dtype=jnp.int32)[None, :]
    live_rows = jnp.any(inside, axis=1)
    segment = jnp.where(live_rows, lax.optimization_barrier(jnp.sum(jnp.where(inside, seq_ids, 0), axis=1)), -1)
    positions = jnp.arange(row_count, dtype=jnp.int32)
    allowed = (segment[:, None] == segment[None, :]) & (positions[:, None] >= positions[None, :])
    return (allowed, live_rows.astype(jnp.float32))

def layer(hidden, params, allowed, live_rows):
    gain_one, shift_one, qkv_mat, qv_vec, proj_mat, proj_vec, gain_two, shift_two, up_mat, up_vec, down_mat, down_vec = params
    highest = lax.Precision.HIGHEST
    row_count = hidden.shape[0]
    normed_one = low(layer_norm(hidden, gain_one, shift_one))
    projected = jnp.dot(normed_one, qkv_mat, precision=highest)
    query = rounded_both(projected[:, :D] + qv_vec[:D]).reshape(row_count, H, HD)
    keys = rounded_both(projected[:, D:2 * D]).reshape(row_count, H, HD)
    values = rounded_both(projected[:, 2 * D:] + qv_vec[D:]).reshape(row_count, H, HD)
    scores = low_back(jnp.einsum('qhd,khd->hqk', query, keys, precision=highest) * 0.125)
    scores = jnp.where(allowed[None], scores, -1e+30)
    row_max = lax.optimization_barrier(jnp.max(scores, axis=-1, keepdims=True))
    weights = jnp.exp(scores - row_max)
    probs = weights / lax.optimization_barrier(jnp.sum(weights, axis=-1, keepdims=True))
    attended = jnp.einsum('hqk,khd->qhd', low(probs), values, precision=highest).reshape(row_count, D)
    attended = rounded_both(attended)
    mixed = hidden + low_back(jnp.dot(attended, proj_mat, precision=highest) + proj_vec)
    normed_two = low(layer_norm(mixed, gain_two, shift_two))
    upper = low_back(jnp.dot(normed_two, up_mat, precision=highest) + up_vec)
    activated = low(jax.nn.gelu(upper, approximate=True))
    branch = low_back(jnp.dot(activated, down_mat, precision=highest) + down_vec)
    return (mixed + branch) * live_rows[:, None]

def reference(hidden_in, cotangent, seq_lengths, seq_owner, seq_start, first_gain, first_shift, qkv_weight, qv_bias, proj_weight, proj_bias, second_gain, second_shift, up_weight, up_bias, down_weight, down_bias):
    params = tuple((item.astype(jnp.float32) for item in (first_gain, first_shift, qkv_weight, qv_bias, proj_weight, proj_bias, second_gain, second_shift, up_weight, up_bias, down_weight, down_bias)))
    blocks_in = hidden_in.astype(jnp.float32).reshape(N_FSDP, TOK_DEV, D)
    blocks_cot = cotangent.astype(jnp.float32).reshape(N_FSDP, TOK_DEV, D)

    def step(totals, item):
        device, block_in, block_cot = item
        allowed, live_rows = slot_layout(seq_lengths, seq_owner, seq_start, device, TOK_DEV)
        result, pull = jax.vjp(lambda first, second: layer(first, second, allowed, live_rows), block_in, params)
        grad_in, grad_params = pull(block_cot)
        totals = jax.tree.map(lambda left, right: left + right, totals, grad_params)
        return (totals, (result.astype(jnp.bfloat16), grad_in))
    zeros = tuple((jnp.zeros_like(item) for item in params))
    devices = jnp.arange(N_FSDP, dtype=jnp.int32)
    totals, (outputs, grads_in) = lax.scan(step, zeros, (devices, blocks_in, blocks_cot))
    g_one, s_one, g_qkv, g_qv, g_proj, g_pb, g_two, s_two, g_up, g_ub, g_down, g_db = totals
    return (outputs.reshape(TOKENS, D), grads_in.reshape(TOKENS, D), g_one, s_one, g_qkv, g_qv, g_proj, g_pb, g_two, s_two, g_up, g_ub, g_down, g_db)
```

```python
import functools

import jax
import jax.numpy as jnp
from jax import lax
from jax.experimental import pallas as pl
from jax.experimental.pallas import tpu as pltpu
from jax.sharding import PartitionSpec as P

D = 768
H = 12
HD = 64


def layer_norm(values, gain, shift):
    average = jnp.mean(values, axis=-1, keepdims=True)
    centered = values - average
    variance = jnp.mean(centered * centered, axis=-1, keepdims=True)
    return centered * lax.rsqrt(variance + 1e-05) * gain + shift


def gelu_tanh(values):
    return jax.nn.gelu(values, approximate=True)


def slot_layout(lengths, owners, starts, device, row_count):
    slot_ids = jnp.arange(row_count, dtype=jnp.int32)[:, None]
    inside = (
        (owners[None, :] == device)
        & (slot_ids >= starts[None, :])
        & (slot_ids < (starts + lengths)[None, :])
    )
    seq_ids = jnp.arange(lengths.shape[0], dtype=jnp.int32)[None, :]
    live_rows = jnp.any(inside, axis=1)
    segment = jnp.where(live_rows, jnp.sum(jnp.where(inside, seq_ids, 0), axis=1), -1)
    positions = jnp.arange(row_count, dtype=jnp.int32)
    allowed = (segment[:, None] == segment[None, :]) & (positions[:, None] >= positions[None, :])
    return (allowed, live_rows.astype(jnp.float32))


def masked_scores(query, keys, allowed):
    scores = jnp.einsum("qhd,khd->hqk", query, keys, preferred_element_type=jnp.float32) * 0.125
    return jnp.where(allowed[None], scores, -1e30)


MESH = pl.DeviceIdType.MESH


def place(grid):
    zs, ys, xs, cs = grid
    me = lax.axis_index("fsdp")
    core = lax.rem(me, cs)
    x = lax.rem(me // cs, xs)
    y = lax.rem(me // (cs * xs), ys)
    z = me // (cs * xs * ys)

    def index(z, y, x, c):
        return ((z * ys + y) * xs + x) * cs + c

    return z, y, x, core, index


def peers_of(grid):
    z, y, x, c, index = place(grid)
    zs = grid[0]
    along_z = [index(lax.rem(z + d, zs), y, x, c) for d in range(1, zs)]
    return along_z, index(z, 1 - y, x, c), index(z, y, 1 - x, c), index(z, y, x, 1 - c)


def greet(grid):
    along_z, ypeer, xpeer, sibling = peers_of(grid)
    barrier = pltpu.get_barrier_semaphore()
    everyone = along_z + [ypeer, xpeer, sibling]
    for peer in everyone:
        pl.semaphore_signal(barrier, inc=1, device_id=(peer,), device_id_type=MESH)
    pl.semaphore_wait(barrier, len(everyone))


def gather_kernel(grid, count, *refs):
    shards, outs = refs[:count], refs[count : 2 * count]
    send, recv, local = refs[2 * count :]
    zs = grid[0]
    z, y, x, c, _ = place(grid)
    along_z, ypeer, xpeer, sibling = peers_of(grid)
    greet(grid)

    def remote(w, slot, src, dst, peer):
        return pltpu.make_async_remote_copy(
            src_ref=src,
            dst_ref=dst,
            send_sem=send.at[w, slot],
            recv_sem=recv.at[w, slot],
            device_id=(peer,),
            device_id_type=MESH,
        )

    started = []

    def go(w, slot, src, dst, peer):
        copy = remote(w, slot, src, dst, peer)
        copy.start()
        started.append(copy)
        return copy

    state = [dict() for _ in range(count)]

    def stage0(w):
        own = pltpu.make_async_copy(shards[w], outs[w].at[z, y, x, c], local.at[w])
        own.start()
        state[w]["own"] = own
        state[w]["z"] = [
            go(w, d, shards[w], outs[w].at[z, y, x, c], peer) for d, peer in enumerate(along_z)
        ]

    def halves(w):
        half = outs[w].shape[-1] // 2
        return pl.ds(0, half), pl.ds(half, half)

    def same(w, slot, where, peer):
        part = outs[w].at[where]
        return go(w, slot, part, part, peer)

    k = zs - 1
    every = slice(None)

    def stage1(w):
        first, second = halves(w)
        for copy in state[w]["z"]:
            copy.wait_recv()
        state[w]["own"].wait()
        state[w]["a"] = same(w, k, (every, y, x, c, every, first), xpeer)
        state[w]["b"] = same(w, k + 1, (every, y, x, c, every, second), ypeer)
        state[w]["s"] = [same(w, k + 2, (every, y, x, c), sibling)]

    def stage2(w):
        first, second = halves(w)
        state[w]["a"].wait_recv()
        a = same(w, k + 3, (every, y, every, c, every, first), ypeer)
        state[w]["b"].wait_recv()
        b = same(w, k + 4, (every, every, x, c, every, second), xpeer)
        state[w]["a"], state[w]["b"] = a, b
        state[w]["s"].append(same(w, k + 5, (every, y, 1 - x, c, every, first), sibling))
        state[w]["s"].append(same(w, k + 6, (every, 1 - y, x, c, every, second), sibling))

    def stage3(w):
        first, second = halves(w)
        state[w]["a"].wait_recv()
        state[w]["s"].append(same(w, k + 7, (every, 1 - y, every, c, every, first), sibling))
        state[w]["b"].wait_recv()
        state[w]["s"].append(same(w, k + 8, (every, every, 1 - x, c, every, second), sibling))

    for w in range(count):
        stage0(w)
    for step in range(count + 2):
        for stage, behind in ((stage3, 2), (stage2, 1), (stage1, 0)):
            if 0 <= step - behind < count:
                stage(step - behind)
    for w in range(count):
        for copy in state[w]["s"]:
            copy.wait_recv()
    for copy in started:
        copy.wait_send()


def gather_all(grid, shards):
    count = len(shards)
    slots = grid[0] - 1 + 9
    return pl.pallas_call(
        functools.partial(gather_kernel, grid, count),
        out_shape=[jax.ShapeDtypeStruct(grid + s.shape, s.dtype) for s in shards],
        in_specs=[pl.BlockSpec(memory_space=pl.ANY)] * count,
        out_specs=[pl.BlockSpec(memory_space=pl.ANY)] * count,
        scratch_shapes=[
            pltpu.SemaphoreType.DMA((count, slots)),
            pltpu.SemaphoreType.DMA((count, slots)),
            pltpu.SemaphoreType.DMA((count,)),
        ],
        compiler_params=pltpu.CompilerParams(collective_id=0, has_side_effects=True),
    )(*shards)


def reduce_kernel(grid, count, *refs):
    lefts, rights, small = refs[:count], refs[count : 2 * count], refs[2 * count]
    total = count + 1
    refs = refs[2 * count + 1 :]
    outs, refs = refs[:total], refs[total:]
    sums, refs = refs[:total], refs[total:]
    got_core, refs = refs[:total], refs[total:]
    got_a1, got_b1, refs = refs[:total], refs[total : 2 * total], refs[2 * total :]
    got_a2, got_b2, refs = refs[:total], refs[total : 2 * total], refs[2 * total :]
    got_z, refs = refs[:total], refs[total:]
    send, recv = refs
    zs, ys, xs, cs = grid
    z, y, x, c, _ = place(grid)
    along_z, ypeer, xpeer, sibling = peers_of(grid)
    greet(grid)
    single = jnp.float32
    started = []
    state = [dict() for _ in range(total)]
    every = slice(None)

    def go(w, slot, src, dst, peer):
        copy = pltpu.make_async_remote_copy(
            src_ref=src,
            dst_ref=dst,
            send_sem=send.at[w, slot],
            recv_sem=recv.at[w, slot],
            device_id=(peer,),
            device_id_type=MESH,
        )
        copy.start()
        started.append(copy)
        return copy

    def halves(w):
        half = sums[w].shape[-1] // 2
        return pl.ds(0, half), pl.ds(half, half)

    def compute(w):
        if w == count:
            sums[w][...] = small[...]
        else:
            left, right = lefts[w], rights[w]
            height, width = sums[w].shape[-2:]
            owners = 384 // height
            zy = owners // (xs * cs)
            for start in range(0, width, 768):

                @pl.loop(0, zs * ys // zy)
                def _(step):
                    rows = left[:, pl.ds(pl.multiple_of(step * 384, 128), 384)]
                    block = lax.dot_general(
                        rows,
                        right[:, start : start + 768],
                        (((0,), (0,)), ((), ())),
                        preferred_element_type=single,
                    ).reshape(zy, xs, cs, height, 768)
                    block = block.astype(sums[w].dtype)
                    for part in range(zy):
                        flat = step * zy + part
                        sums[w][flat // ys, lax.rem(flat, ys), :, :, :, start : start + 768] = block[part]

        state[w]["s"] = go(w, 0, sums[w].at[:, :, :, 1 - c], got_core[w], sibling)

    def add(w, mine, other):
        value = sums[w][mine].astype(single) + other.astype(single)
        sums[w][mine] = value.astype(sums[w].dtype)

    def stage1(w):
        first, second = halves(w)
        state[w]["s"].wait_recv()

        @pl.loop(0, zs * ys)
        def _(step):
            zz, yy = step // ys, lax.rem(step, ys)
            for xx in range(xs):
                add(w, (zz, yy, xx, c), got_core[w][zz, yy, xx])

        state[w]["a"] = go(w, 1, sums[w].at[:, 1 - y, :, c, :, first], got_a1[w], ypeer)
        state[w]["b"] = go(w, 2, sums[w].at[:, :, 1 - x, c, :, second], got_b1[w], xpeer)

    def stage2(w):
        first, second = halves(w)
        state[w]["a"].wait_recv()

        @pl.loop(0, zs)
        def _(zz):
            for xx in range(xs):
                add(w, (zz, y, xx, c, every, first), got_a1[w][zz, xx])

        a = go(w, 3, sums[w].at[:, y, 1 - x, c, :, first], got_a2[w], xpeer)
        state[w]["b"].wait_recv()

        @pl.loop(0, zs)
        def _(zz):
            for yy in range(ys):
                add(w, (zz, yy, x, c, every, second), got_b1[w][zz, yy])

        b = go(w, 4, sums[w].at[:, 1 - y, x, c, :, second], got_b2[w], ypeer)
        state[w]["a"], state[w]["b"] = a, b

    def stage3(w):
        first, second = halves(w)
        state[w]["a"].wait_recv()
        state[w]["b"].wait_recv()

        @pl.loop(0, zs)
        def _(zz):
            add(w, (zz, y, x, c, every, first), got_a2[w][zz])
            add(w, (zz, y, x, c, every, second), got_b2[w][zz])

        state[w]["z"] = [
            go(w, 5 + d, sums[w].at[lax.rem(z + d + 1, zs), y, x, c], got_z[w].at[d], peer)
            for d, peer in enumerate(along_z)
        ]

    def stage4(w):
        value = sums[w][z, y, x, c].astype(single)
        for d, copy in enumerate(state[w]["z"]):
            copy.wait_recv()
            value = value + got_z[w][d].astype(single)
        outs[w][...] = value

    stages = ((stage4, 4), (stage3, 3), (stage2, 2), (stage1, 1), (compute, 0))
    for step in range(total + 4):
        for stage, behind in stages:
            if 0 <= step - behind < total:
                stage(step - behind)
    for copy in started:
        copy.wait_send()


def reduce_all(grid, pairs, small):
    half = jnp.bfloat16
    count = len(pairs)
    devices = grid[0] * grid[1] * grid[2] * grid[3]
    zs, ys, xs, _ = grid
    shapes = [(left.shape[1] // devices, right.shape[1], half) for left, right in pairs]
    shapes.append((small.shape[-2], small.shape[-1], small.dtype))

    def scratch(lead, part=1):
        return [pltpu.VMEM(lead + (r, n // part), dtype) for r, n, dtype in shapes]

    slots = 5 + zs - 1
    vmem = pl.BlockSpec(memory_space=pltpu.VMEM)
    return pl.pallas_call(
        functools.partial(reduce_kernel, grid, count),
        out_shape=[jax.ShapeDtypeStruct((r, n), jnp.float32) for r, n, _ in shapes],
        in_specs=[vmem] * (2 * count + 1),
        out_specs=[vmem] * (count + 1),
        scratch_shapes=(
            scratch(grid)
            + scratch((zs, ys, xs))
            + scratch((zs, xs), 2)
            + scratch((zs, ys), 2)
            + scratch((zs,), 2)
            + scratch((zs,), 2)
            + scratch((zs - 1,))
            + [
                pltpu.SemaphoreType.DMA((count + 1, slots)),
                pltpu.SemaphoreType.DMA((count + 1, slots)),
            ]
        ),
        compiler_params=pltpu.CompilerParams(
            collective_id=1, has_side_effects=True, vmem_limit_bytes=60 * 2**20
        ),
    )(*[left for left, _ in pairs], *[right for _, right in pairs], small)


def grid_of(devices, matrices):
    rest = devices // 8
    if devices % 8 or rest < 2 or any(m.shape[0] % 8 for m in matrices):
        return None
    return (rest, 2, 2, 2)


def per_device(
    devices,
    hidden_in,
    cotangent,
    seq_lengths,
    seq_owner,
    seq_start,
    first_gain,
    first_shift,
    qkv_weight,
    qv_bias,
    proj_weight,
    proj_bias,
    second_gain,
    second_shift,
    up_weight,
    up_bias,
    down_weight,
    down_bias,
):
    single = jnp.float32
    half = jnp.bfloat16
    matrices = (qkv_weight, proj_weight, up_weight, down_weight)
    vectors = (
        first_gain,
        first_shift,
        qv_bias,
        proj_bias,
        second_gain,
        second_shift,
        up_bias,
        down_bias,
    )
    grid = grid_of(devices, matrices)
    packed = jnp.concatenate(vectors)
    used = packed.shape[0]
    if grid is None:
        mats = [lax.all_gather(m, "fsdp", axis=0, tiled=True) for m in matrices]
        vecs = lax.all_gather(packed, "fsdp", axis=0)
    else:
        packed = jnp.pad(packed, (0, 4096 - used)).reshape(16, 256)
        vecs, *mats = gather_all(grid, (packed,) + matrices)
        mats = [m.reshape(-1, m.shape[-1]) for m in mats]
        vecs = vecs.reshape(devices, 4096)
    qkv_mat, proj_mat, up_mat, down_mat = mats
    cuts, at = [], 0
    for v in vectors:
        cuts.append(vecs[:, at : at + v.shape[0]].reshape(-1))
        at += v.shape[0]
    gain_one, shift_one, qv_vec, proj_vec, gain_two, shift_two, up_vec, down_vec = cuts
    row_count = hidden_in.shape[0]
    allowed, live_rows = slot_layout(
        seq_lengths, seq_owner, seq_start, lax.axis_index("fsdp"), row_count
    )
    inputs = hidden_in.astype(single)
    normed_f, norm_pull_one = jax.vjp(
        layer_norm, inputs, gain_one.astype(single), shift_one.astype(single)
    )
    normed_one = normed_f.astype(half)
    projected = jnp.dot(normed_one, qkv_mat, preferred_element_type=single)
    qv_float = qv_vec.astype(single)
    query = (projected[:, :D] + qv_float[:D]).astype(half).reshape(row_count, H, HD)
    keys = projected[:, D : 2 * D].astype(half).reshape(row_count, H, HD)
    values = (projected[:, 2 * D :] + qv_float[D:]).astype(half).reshape(row_count, H, HD)
    scores = masked_scores(query, keys, allowed)
    row_max = jnp.max(scores, axis=-1, keepdims=True)
    weights = jnp.exp(scores - row_max)
    row_total = jnp.sum(weights, axis=-1, keepdims=True)
    probs = weights / row_total
    log_total = row_max + jnp.log(row_total)
    attended = jnp.einsum("hqk,khd->qhd", probs.astype(half), values, preferred_element_type=single)
    attended = attended.reshape(row_count, D).astype(half)
    mixed = (
        inputs
        + jnp.dot(attended, proj_mat, preferred_element_type=single)
        + proj_vec.astype(single)
    )
    normed_g, norm_pull_two = jax.vjp(
        layer_norm, mixed, gain_two.astype(single), shift_two.astype(single)
    )
    normed_two = normed_g.astype(half)
    upper = jnp.dot(normed_two, up_mat, preferred_element_type=single) + up_vec.astype(single)
    active_f, gelu_pull = jax.vjp(gelu_tanh, upper)
    activated = active_f.astype(half)
    branch = jnp.dot(activated, down_mat, preferred_element_type=single) + down_vec.astype(single)
    layer_out = ((mixed + branch) * live_rows[:, None]).astype(half)
    qkv_back, proj_back, up_back, down_back = qkv_mat, proj_mat, up_mat, down_mat
    grad_out = cotangent.astype(single) * live_rows[:, None]
    grad_branch = grad_out.astype(half)
    down_bias_grad = jnp.sum(grad_branch.astype(single), axis=0)
    grad_active = jnp.einsum("td,fd->tf", grad_branch, down_back, preferred_element_type=single)
    grad_upper = gelu_pull(grad_active)[0].astype(half)
    up_bias_grad = jnp.sum(grad_upper.astype(single), axis=0)
    grad_normed_two = jnp.einsum("tf,df->td", grad_upper, up_back, preferred_element_type=single)
    grad_mixed_norm, second_gain_grad, second_shift_grad = norm_pull_two(grad_normed_two)
    grad_mixed = grad_out + grad_mixed_norm
    grad_proj = grad_mixed.astype(half)
    proj_bias_grad = jnp.sum(grad_proj.astype(single), axis=0)
    grad_attended = jnp.einsum("td,ed->te", grad_proj, proj_back, preferred_element_type=single)
    grad_attended = grad_attended.astype(half).reshape(row_count, H, HD)
    probs_again = jnp.exp(masked_scores(query, keys, allowed) - log_total)
    grad_probs = jnp.einsum("qhd,khd->hqk", grad_attended, values, preferred_element_type=single)
    row_delta = jnp.sum(probs_again * grad_probs, axis=-1, keepdims=True)
    grad_scores = (probs_again * (grad_probs - row_delta)).astype(half)
    grad_query = (
        jnp.einsum("hqk,khd->qhd", grad_scores, keys, preferred_element_type=single) * 0.125
    ).astype(half)
    grad_keys = (
        jnp.einsum("hqk,qhd->khd", grad_scores, query, preferred_element_type=single) * 0.125
    ).astype(half)
    grad_values = jnp.einsum(
        "hqk,qhd->khd", probs_again.astype(half), grad_attended, preferred_element_type=single
    ).astype(half)
    grad_projected = jnp.concatenate(
        [
            grad_query.reshape(row_count, D),
            grad_keys.reshape(row_count, D),
            grad_values.reshape(row_count, D),
        ],
        axis=1,
    )
    qv_bias_grad = jnp.concatenate(
        [
            jnp.sum(grad_query.reshape(row_count, D).astype(single), axis=0),
            jnp.sum(grad_values.reshape(row_count, D).astype(single), axis=0),
        ]
    )
    grad_normed_one = jnp.einsum(
        "te,de->td", grad_projected, qkv_back, preferred_element_type=single
    )
    grad_input_norm, first_gain_grad, first_shift_grad = norm_pull_one(grad_normed_one)
    input_grad = grad_mixed + grad_input_norm
    vector_grads = (
        first_gain_grad,
        first_shift_grad,
        qv_bias_grad,
        proj_bias_grad,
        second_gain_grad,
        second_shift_grad,
        up_bias_grad,
        down_bias_grad,
    )
    small = jnp.concatenate([v.reshape(devices, -1) for v in vector_grads], axis=1)
    pairs = (
        (activated, grad_branch),
        (normed_two, grad_upper),
        (normed_one, grad_projected),
        (attended, grad_proj),
    )
    if grid is None:
        sums = [
            lax.psum_scatter(
                jnp.einsum("tm,tn->mn", left, right, preferred_element_type=single),
                "fsdp",
                scatter_dimension=0,
                tiled=True,
            )
            for left, right in pairs
        ]
        small = lax.psum_scatter(small, "fsdp", scatter_dimension=0, tiled=True)
        down_sum, up_sum, qkv_sum, proj_sum = sums
    else:
        small = jnp.pad(small, ((0, 0), (0, 2048 - used))).reshape(grid + (8, 256))
        down_sum, up_sum, qkv_sum, proj_sum, small = reduce_all(grid, pairs, small)
    flat = small.reshape(-1)
    cuts, at = [], 0
    for v in vectors:
        cuts.append(flat[at : at + v.shape[0]])
        at += v.shape[0]
    gain_one, shift_one, qv_sum, proj_vec, gain_two, shift_two, up_vec, down_vec = cuts
    return (
        layer_out,
        input_grad,
        gain_one,
        shift_one,
        qkv_sum,
        qv_sum,
        proj_sum,
        proj_vec,
        gain_two,
        shift_two,
        up_sum,
        up_vec,
        down_sum,
        down_vec,
    )


def solution(mesh):
    return jax.shard_map(
        functools.partial(per_device, mesh.shape["fsdp"]),
        mesh=mesh,
        in_specs=(
            P("fsdp", None),
            P("fsdp", None),
            P(),
            P(),
            P(),
            P("fsdp"),
            P("fsdp"),
            P("fsdp", None),
            P("fsdp"),
            P("fsdp", None),
            P("fsdp"),
            P("fsdp"),
            P("fsdp"),
            P("fsdp", None),
            P("fsdp"),
            P("fsdp", None),
            P("fsdp"),
        ),
        out_specs=(
            P("fsdp", None),
            P("fsdp", None),
            P("fsdp"),
            P("fsdp"),
            P("fsdp", None),
            P("fsdp"),
            P("fsdp", None),
            P("fsdp"),
            P("fsdp"),
            P("fsdp"),
            P("fsdp", None),
            P("fsdp"),
            P("fsdp", None),
            P("fsdp"),
        ),
        check_vma=False,
    )
```

```python
import functools

import jax
import jax.numpy as jnp
from jax import lax
from jax.experimental import pallas as pl
from jax.experimental.pallas import tpu as pltpu
from jax.sharding import PartitionSpec as P

D = 768
H = 12
HD = 64


def layer_norm(values, gain, shift):
    average = jnp.mean(values, axis=-1, keepdims=True)
    centered = values - average
    variance = jnp.mean(centered * centered, axis=-1, keepdims=True)
    return centered * lax.rsqrt(variance + 1e-05) * gain + shift


def gelu_tanh(values):
    return jax.nn.gelu(values, approximate=True)


def slot_layout(lengths, owners, starts, device, row_count):
    slot_ids = jnp.arange(row_count, dtype=jnp.int32)[:, None]
    inside = (
        (owners[None, :] == device)
        & (slot_ids >= starts[None, :])
        & (slot_ids < (starts + lengths)[None, :])
    )
    seq_ids = jnp.arange(lengths.shape[0], dtype=jnp.int32)[None, :]
    live_rows = jnp.any(inside, axis=1)
    segment = jnp.where(live_rows, jnp.sum(jnp.where(inside, seq_ids, 0), axis=1), -1)
    positions = jnp.arange(row_count, dtype=jnp.int32)
    allowed = (segment[:, None] == segment[None, :]) & (positions[:, None] >= positions[None, :])
    return (allowed, live_rows.astype(jnp.float32))


def masked_scores(query, keys, allowed):
    scores = jnp.einsum("qhd,khd->hqk", query, keys, preferred_element_type=jnp.float32) * 0.125
    return jnp.where(allowed[None], scores, -1e30)


MESH = pl.DeviceIdType.MESH


def place(grid):
    zs, ys, xs, cs = grid
    me = lax.axis_index("fsdp")
    core = lax.rem(me, cs)
    x = lax.rem(me // cs, xs)
    y = lax.rem(me // (cs * xs), ys)
    z = me // (cs * xs * ys)

    def index(z, y, x, c):
        return ((z * ys + y) * xs + x) * cs + c

    return z, y, x, core, index


def peers_of(grid):
    z, y, x, c, index = place(grid)
    zs = grid[0]
    along_z = [index(lax.rem(z + d, zs), y, x, c) for d in range(1, zs)]
    return along_z, index(z, 1 - y, x, c), index(z, y, 1 - x, c), index(z, y, x, 1 - c)


def greet(grid):
    along_z, ypeer, xpeer, sibling = peers_of(grid)
    barrier = pltpu.get_barrier_semaphore()
    everyone = along_z + [ypeer, xpeer, sibling]
    for peer in everyone:
        pl.semaphore_signal(barrier, inc=1, device_id=(peer,), device_id_type=MESH)
    pl.semaphore_wait(barrier, len(everyone))


def gather_kernel(grid, count, *refs):
    shards, outs = refs[:count], refs[count : 2 * count]
    send, recv, local = refs[2 * count :]
    zs = grid[0]
    z, y, x, c, _ = place(grid)
    along_z, ypeer, xpeer, sibling = peers_of(grid)
    greet(grid)

    def remote(w, slot, src, dst, peer):
        return pltpu.make_async_remote_copy(
            src_ref=src,
            dst_ref=dst,
            send_sem=send.at[w, slot],
            recv_sem=recv.at[w, slot],
            device_id=(peer,),
            device_id_type=MESH,
        )

    started = []

    def go(w, slot, src, dst, peer):
        copy = remote(w, slot, src, dst, peer)
        copy.start()
        started.append(copy)
        return copy

    state = [dict() for _ in range(count)]
    every = slice(None)

    def same(w, slot, where, peer):
        part = outs[w].at[where]
        return go(w, slot, part, part, peer)

    first_x, first_y, first_s, rest = zs - 1, 2 * zs - 1, 3 * zs - 1, 4 * zs - 1

    def stage0(w):
        mine = outs[w].at[z, y, x, c]
        own = pltpu.make_async_copy(shards[w], mine, local.at[w])
        own.start()
        state[w]["own"] = own
        state[w]["x"] = [go(w, first_x, shards[w], mine, xpeer)]
        state[w]["y"] = [go(w, first_y, shards[w], mine, ypeer)]
        state[w]["z"] = [go(w, d, shards[w], mine, peer) for d, peer in enumerate(along_z)]
        state[w]["s"] = [go(w, first_s, shards[w], mine, sibling)]

    def stage1(w):
        for d, copy in enumerate(state[w]["z"]):
            copy.wait_recv()
            block = (lax.rem(z + zs - 1 - d, zs), y, x, c)
            state[w]["x"].append(same(w, first_x + 1 + d, block, xpeer))
            state[w]["y"].append(same(w, first_y + 1 + d, block, ypeer))
            state[w]["s"].append(same(w, first_s + 1 + d, block, sibling))
        if w + 2 < count:
            stage0(w + 2)

    def stage2(w):
        half = outs[w].shape[-1] // 2
        for copy in state[w]["x"]:
            copy.wait_recv()
        a = same(w, rest, (every, y, 1 - x, c, every, pl.ds(0, half)), ypeer)
        for copy in state[w]["y"]:
            copy.wait_recv()
        b = same(w, rest + 1, (every, 1 - y, x, c, every, pl.ds(half, half)), xpeer)
        state[w]["d"] = [a, b]
        state[w]["s"].append(same(w, rest + 2, (every, y, 1 - x, c), sibling))
        state[w]["s"].append(same(w, rest + 3, (every, 1 - y, x, c), sibling))

    def stage3(w):
        for copy in state[w]["d"]:
            copy.wait_recv()
        state[w]["s"].append(same(w, rest + 4, (every, 1 - y, 1 - x, c), sibling))

    stage0(0)
    stage0(1)
    for step in range(count + 2):
        for stage, behind in ((stage1, 0), (stage2, 1), (stage3, 2)):
            if 0 <= step - behind < count:
                stage(step - behind)
    for w in range(count):
        state[w]["own"].wait()
        for copy in state[w]["s"]:
            copy.wait_recv()
    for copy in started:
        copy.wait_send()


def gather_all(grid, shards):
    count = len(shards)
    slots = 4 * grid[0] + 4
    return pl.pallas_call(
        functools.partial(gather_kernel, grid, count),
        out_shape=[jax.ShapeDtypeStruct(grid + s.shape, s.dtype) for s in shards],
        in_specs=[pl.BlockSpec(memory_space=pl.ANY)] * count,
        out_specs=[pl.BlockSpec(memory_space=pl.ANY)] * count,
        scratch_shapes=[
            pltpu.SemaphoreType.DMA((count, slots)),
            pltpu.SemaphoreType.DMA((count, slots)),
            pltpu.SemaphoreType.DMA((count,)),
        ],
        compiler_params=pltpu.CompilerParams(collective_id=0, has_side_effects=True),
    )(*shards)


def reduce_kernel(grid, pieces, count, *refs):
    lefts, rights, small = refs[:count], refs[count : 2 * count], refs[2 * count]
    refs = refs[2 * count + 1 :]
    outs, refs = refs[: count + 1], refs[count + 1 :]
    total = len(pieces) + 1
    sums, refs = refs[:total], refs[total:]
    got_core, refs = refs[:total], refs[total:]
    got_a1, got_b1, refs = refs[:total], refs[total : 2 * total], refs[2 * total :]
    got_a2, got_b2, refs = refs[:total], refs[total : 2 * total], refs[2 * total :]
    got_z, refs = refs[:total], refs[total:]
    send, recv = refs
    zs, ys, xs, cs = grid
    z, y, x, c, _ = place(grid)
    along_z, ypeer, xpeer, sibling = peers_of(grid)
    greet(grid)
    single = jnp.float32
    started = []
    state = [dict() for _ in range(total)]
    every = slice(None)

    def go(w, slot, src, dst, peer):
        copy = pltpu.make_async_remote_copy(
            src_ref=src,
            dst_ref=dst,
            send_sem=send.at[w, slot],
            recv_sem=recv.at[w, slot],
            device_id=(peer,),
            device_id_type=MESH,
        )
        copy.start()
        started.append(copy)
        return copy

    def halves(w):
        half = sums[w].shape[-1] // 2
        return pl.ds(0, half), pl.ds(half, half)

    def compute(w):
        if w == total - 1:
            sums[w][...] = small[...]
        else:
            product, first, width = pieces[w]
            left, right = lefts[product], rights[product]
            height = sums[w].shape[-2]
            zy = 384 // height // (xs * cs)

            @pl.loop(0, zs * ys // zy)
            def _(step):
                rows = left[:, pl.ds(pl.multiple_of(step * 384, 128), 384)].T
                for start in range(0, width, 256):
                    block = jnp.dot(
                        rows,
                        right[:, first + start : first + start + 256],
                        preferred_element_type=single,
                    )
                    block = block.reshape(zy, xs, cs, height, 256).astype(sums[w].dtype)
                    for part in range(zy):
                        flat = step * zy + part
                        zz, yy = flat // ys, lax.rem(flat, ys)
                        sums[w][zz, yy, :, :, :, start : start + 256] = block[part]

        state[w]["s"] = go(w, 0, sums[w].at[:, :, :, 1 - c], got_core[w], sibling)

    def add(w, mine, other):
        value = sums[w][mine].astype(single) + other.astype(single)
        sums[w][mine] = value.astype(sums[w].dtype)

    def stage1(w):
        first, second = halves(w)
        state[w]["s"].wait_recv()

        @pl.loop(0, zs * ys)
        def _(step):
            zz, yy = step // ys, lax.rem(step, ys)
            for xx in range(xs):
                add(w, (zz, yy, xx, c), got_core[w][zz, yy, xx])

        state[w]["a"] = go(w, 1, sums[w].at[:, 1 - y, :, c, :, first], got_a1[w], ypeer)
        state[w]["b"] = go(w, 2, sums[w].at[:, :, 1 - x, c, :, second], got_b1[w], xpeer)

    def stage2(w):
        first, second = halves(w)
        state[w]["a"].wait_recv()

        @pl.loop(0, zs)
        def _(zz):
            for xx in range(xs):
                add(w, (zz, y, xx, c, every, first), got_a1[w][zz, xx])

        a = go(w, 3, sums[w].at[:, y, 1 - x, c, :, first], got_a2[w], xpeer)
        state[w]["b"].wait_recv()

        @pl.loop(0, zs)
        def _(zz):
            for yy in range(ys):
                add(w, (zz, yy, x, c, every, second), got_b1[w][zz, yy])

        b = go(w, 4, sums[w].at[:, 1 - y, x, c, :, second], got_b2[w], ypeer)
        state[w]["a"], state[w]["b"] = a, b

    def stage3(w):
        first, second = halves(w)
        state[w]["a"].wait_recv()
        state[w]["b"].wait_recv()

        @pl.loop(0, zs)
        def _(zz):
            add(w, (zz, y, x, c, every, first), got_a2[w][zz])
            add(w, (zz, y, x, c, every, second), got_b2[w][zz])

        state[w]["z"] = [
            go(w, 5 + d, sums[w].at[lax.rem(z + d + 1, zs), y, x, c], got_z[w].at[d], peer)
            for d, peer in enumerate(along_z)
        ]

    def stage4(w):
        value = sums[w][z, y, x, c].astype(single)
        for d, copy in enumerate(state[w]["z"]):
            copy.wait_recv()
            value = value + got_z[w][d].astype(single)
        if w == total - 1:
            outs[count][...] = value
        else:
            product, first, width = pieces[w]
            outs[product][:, first : first + width] = value

    stages = ((compute, 0), (stage1, 1), (stage2, 2), (stage3, 3), (stage4, 4))
    for step in range(total + 4):
        for stage, behind in stages:
            if 0 <= step - behind < total:
                stage(step - behind)
    for copy in started:
        copy.wait_send()


def reduce_all(grid, pairs, small):
    half = jnp.bfloat16
    count = len(pairs)
    devices = grid[0] * grid[1] * grid[2] * grid[3]
    zs, ys, xs, _ = grid
    sizes = [(left.shape[1] // devices, right.shape[1]) for left, right in pairs]
    pieces = []
    for product, (_, columns) in enumerate(sizes):
        parts = 1 if columns == 768 and sizes[product][0] < 96 else 2
        width = columns // parts
        width = -(-width // 256) * 256
        for first in range(0, columns, width):
            pieces.append((product, first, min(width, columns - first)))
    shapes = [(sizes[product][0], width, half) for product, _, width in pieces]
    shapes.append((small.shape[-2], small.shape[-1], small.dtype))
    total = len(shapes)
    results = sizes + [small.shape[-2:]]

    def scratch(lead, part=1):
        return [pltpu.VMEM(lead + (r, n // part), dtype) for r, n, dtype in shapes]

    slots = 5 + zs - 1
    vmem = pl.BlockSpec(memory_space=pltpu.VMEM)
    return pl.pallas_call(
        functools.partial(reduce_kernel, grid, tuple(pieces), count),
        out_shape=[jax.ShapeDtypeStruct(size, jnp.float32) for size in results],
        in_specs=[vmem] * (2 * count + 1),
        out_specs=[vmem] * (count + 1),
        scratch_shapes=(
            scratch(grid)
            + scratch((zs, ys, xs))
            + scratch((zs, xs), 2)
            + scratch((zs, ys), 2)
            + scratch((zs,), 2)
            + scratch((zs,), 2)
            + scratch((zs - 1,))
            + [
                pltpu.SemaphoreType.DMA((total, slots)),
                pltpu.SemaphoreType.DMA((total, slots)),
            ]
        ),
        compiler_params=pltpu.CompilerParams(
            collective_id=1, has_side_effects=True, vmem_limit_bytes=60 * 2**20
        ),
    )(*[left for left, _ in pairs], *[right for _, right in pairs], small)


def grid_of(devices, matrices):
    rest = devices // 8
    if devices % 8 or rest < 2 or any(m.shape[0] % 8 for m in matrices):
        return None
    return (rest, 2, 2, 2)


def per_device(
    devices,
    hidden_in,
    cotangent,
    seq_lengths,
    seq_owner,
    seq_start,
    first_gain,
    first_shift,
    qkv_weight,
    qv_bias,
    proj_weight,
    proj_bias,
    second_gain,
    second_shift,
    up_weight,
    up_bias,
    down_weight,
    down_bias,
):
    single = jnp.float32
    half = jnp.bfloat16
    matrices = (qkv_weight, proj_weight, up_weight, down_weight)
    vectors = (
        first_gain,
        first_shift,
        qv_bias,
        proj_bias,
        second_gain,
        second_shift,
        up_bias,
        down_bias,
    )
    grid = grid_of(devices, matrices)
    unit = first_gain.shape[0]
    packed = jnp.concatenate([v.reshape(-1, unit) for v in vectors])
    lines = packed.shape[0]
    used = lines * unit
    if grid is None:
        mats = [lax.all_gather(m, "fsdp", axis=0, tiled=True) for m in matrices]
        vecs = lax.all_gather(packed, "fsdp", axis=0)
    else:
        packed = jnp.pad(packed, ((0, 16 - lines), (0, 256 - unit)))
        order = (packed, proj_weight, qkv_weight, up_weight)
        down_full = lax.all_gather(down_weight, "fsdp", axis=0, tiled=True)
        vecs, *mats = gather_all(grid, order)
        proj_full, qkv_full, up_full = [m.reshape(-1, m.shape[-1]) for m in mats]
        mats = (qkv_full, proj_full, up_full, down_full)
        vecs = vecs.reshape(devices, 16, 256)[:, :lines, :unit]
    qkv_mat, proj_mat, up_mat, down_mat = mats
    cuts, at = [], 0
    for v in vectors:
        cuts.append(vecs[:, at : at + v.shape[0] // unit].reshape(-1))
        at += v.shape[0] // unit
    gain_one, shift_one, qv_vec, proj_vec, gain_two, shift_two, up_vec, down_vec = cuts
    row_count = hidden_in.shape[0]
    allowed, live_rows = slot_layout(
        seq_lengths, seq_owner, seq_start, lax.axis_index("fsdp"), row_count
    )
    inputs = hidden_in.astype(single)
    normed_f, norm_pull_one = jax.vjp(
        layer_norm, inputs, gain_one.astype(single), shift_one.astype(single)
    )
    normed_one = normed_f.astype(half)
    projected = jnp.dot(normed_one, qkv_mat, preferred_element_type=single)
    qv_float = qv_vec.astype(single)
    query = (projected[:, :D] + qv_float[:D]).astype(half).reshape(row_count, H, HD)
    keys = projected[:, D : 2 * D].astype(half).reshape(row_count, H, HD)
    values = (projected[:, 2 * D :] + qv_float[D:]).astype(half).reshape(row_count, H, HD)
    scores = masked_scores(query, keys, allowed)
    row_max = jnp.max(scores, axis=-1, keepdims=True)
    weights = jnp.exp(scores - row_max)
    row_total = jnp.sum(weights, axis=-1, keepdims=True)
    probs = weights / row_total
    log_total = row_max + jnp.log(row_total)
    attended = jnp.einsum("hqk,khd->qhd", probs.astype(half), values, preferred_element_type=single)
    attended = attended.reshape(row_count, D).astype(half)
    mixed = (
        inputs
        + jnp.dot(attended, proj_mat, preferred_element_type=single)
        + proj_vec.astype(single)
    )
    normed_g, norm_pull_two = jax.vjp(
        layer_norm, mixed, gain_two.astype(single), shift_two.astype(single)
    )
    normed_two = normed_g.astype(half)
    upper = jnp.dot(normed_two, up_mat, preferred_element_type=single) + up_vec.astype(single)
    active_f, gelu_pull = jax.vjp(gelu_tanh, upper)
    activated = active_f.astype(half)
    branch = jnp.dot(activated, down_mat, preferred_element_type=single) + down_vec.astype(single)
    layer_out = ((mixed + branch) * live_rows[:, None]).astype(half)
    qkv_back, proj_back, up_back, down_back = qkv_mat, proj_mat, up_mat, down_mat
    grad_out = cotangent.astype(single) * live_rows[:, None]
    grad_branch = grad_out.astype(half)
    down_bias_grad = jnp.sum(grad_branch.astype(single), axis=0)
    grad_active = jnp.einsum("td,fd->tf", grad_branch, down_back, preferred_element_type=single)
    grad_upper = gelu_pull(grad_active)[0].astype(half)
    up_bias_grad = jnp.sum(grad_upper.astype(single), axis=0)
    grad_normed_two = jnp.einsum("tf,df->td", grad_upper, up_back, preferred_element_type=single)
    grad_mixed_norm, second_gain_grad, second_shift_grad = norm_pull_two(grad_normed_two)
    grad_mixed = grad_out + grad_mixed_norm
    grad_proj = grad_mixed.astype(half)
    proj_bias_grad = jnp.sum(grad_proj.astype(single), axis=0)
    grad_attended = jnp.einsum("td,ed->te", grad_proj, proj_back, preferred_element_type=single)
    grad_attended = grad_attended.astype(half).reshape(row_count, H, HD)
    probs_again = jnp.exp(masked_scores(query, keys, allowed) - log_total)
    grad_probs = jnp.einsum("qhd,khd->hqk", grad_attended, values, preferred_element_type=single)
    row_delta = jnp.sum(probs_again * grad_probs, axis=-1, keepdims=True)
    grad_scores = (probs_again * (grad_probs - row_delta)).astype(half)
    grad_query = (
        jnp.einsum("hqk,khd->qhd", grad_scores, keys, preferred_element_type=single) * 0.125
    ).astype(half)
    grad_keys = (
        jnp.einsum("hqk,qhd->khd", grad_scores, query, preferred_element_type=single) * 0.125
    ).astype(half)
    grad_values = jnp.einsum(
        "hqk,qhd->khd", probs_again.astype(half), grad_attended, preferred_element_type=single
    ).astype(half)
    grad_projected = jnp.concatenate(
        [
            grad_query.reshape(row_count, D),
            grad_keys.reshape(row_count, D),
            grad_values.reshape(row_count, D),
        ],
        axis=1,
    )
    qv_bias_grad = jnp.concatenate(
        [
            jnp.sum(grad_query.reshape(row_count, D).astype(single), axis=0),
            jnp.sum(grad_values.reshape(row_count, D).astype(single), axis=0),
        ]
    )
    grad_normed_one = jnp.einsum(
        "te,de->td", grad_projected, qkv_back, preferred_element_type=single
    )
    grad_input_norm, first_gain_grad, first_shift_grad = norm_pull_one(grad_normed_one)
    input_grad = grad_mixed + grad_input_norm
    vector_grads = (
        first_gain_grad,
        first_shift_grad,
        qv_bias_grad,
        proj_bias_grad,
        second_gain_grad,
        second_shift_grad,
        up_bias_grad,
        down_bias_grad,
    )
    small = jnp.concatenate([v.reshape(devices, -1) for v in vector_grads], axis=1)
    pairs = (
        (activated, grad_branch),
        (normed_two, grad_upper),
        (normed_one, grad_projected),
        (attended, grad_proj),
    )
    if grid is None:
        sums = [
            lax.psum_scatter(
                jnp.einsum("tm,tn->mn", left, right, preferred_element_type=single),
                "fsdp",
                scatter_dimension=0,
                tiled=True,
            )
            for left, right in pairs
        ]
        small = lax.psum_scatter(small, "fsdp", scatter_dimension=0, tiled=True)
        down_sum, up_sum, qkv_sum, proj_sum = sums
    else:
        small = jnp.pad(small, ((0, 0), (0, 2048 - used))).reshape(grid + (8, 256))
        down_sum, up_sum, qkv_sum, proj_sum, small = reduce_all(grid, pairs, small)
    flat = small.reshape(-1)
    cuts, at = [], 0
    for v in vectors:
        cuts.append(flat[at : at + v.shape[0]])
        at += v.shape[0]
    gain_one, shift_one, qv_sum, proj_vec, gain_two, shift_two, up_vec, down_vec = cuts
    return (
        layer_out,
        input_grad,
        gain_one,
        shift_one,
        qkv_sum,
        qv_sum,
        proj_sum,
        proj_vec,
        gain_two,
        shift_two,
        up_sum,
        up_vec,
        down_sum,
        down_vec,
    )


def solution(mesh):
    return jax.shard_map(
        functools.partial(per_device, mesh.shape["fsdp"]),
        mesh=mesh,
        in_specs=(
            P("fsdp", None),
            P("fsdp", None),
            P(),
            P(),
            P(),
            P("fsdp"),
            P("fsdp"),
            P("fsdp", None),
            P("fsdp"),
            P("fsdp", None),
            P("fsdp"),
            P("fsdp"),
            P("fsdp"),
            P("fsdp", None),
            P("fsdp"),
            P("fsdp", None),
            P("fsdp"),
        ),
        out_specs=(
            P("fsdp", None),
            P("fsdp", None),
            P("fsdp"),
            P("fsdp"),
            P("fsdp", None),
            P("fsdp"),
            P("fsdp", None),
            P("fsdp"),
            P("fsdp"),
            P("fsdp"),
            P("fsdp", None),
            P("fsdp"),
            P("fsdp", None),
            P("fsdp"),
        ),
        check_vma=False,
    )
```
